128 devices in a mesh: freq: 4 (over z), space: 32 (over y, x, core).
Axes of the slice: x: 4, y: 4, z: 4, core: 2. Of those that a mesh axis runs over, the one named last changes fastest.
Arguments:
- segments: bfloat16 [128, 256, 32768], P('freq', None, 'space'), may hold values from -6 to 6
- volumes: float32 [32768], P('space'), may hold values from 0.03 to 3.4, as said below
- freq_bins: int32 [16], replicated, may hold values from 1 to 127, as said below
Outputs:
- modes: float32 [16, 32768, 256], P('freq', 'space')
- triangle: float32 [16, 256, 256], P('freq')
The draws below stay inside these ranges and needn't reach their ends.
Inputs may be any that keep to these rules, and one draw needn't show every extreme that they name: `volumes`: positive weights. `freq_bins`: distinct bins; the first two are 1 and 127.
All inputs are finite; a program needn't handle non-finite values.
Results may differ from the reference program's by a relative error of at most 0.0027.
Values sent between devices are 32-bit elements; how exact they have to be, the bound alone decides.
No kernel may reach another device: no remote copies, remote signals or barrier semaphores. Data moves between devices by JAX's collectives and lax.ppermute only.
A program may use at most 128 MiB of HBM per device.

```python
import math
import jax
import jax.numpy as jnp
from jax import lax

NFFT = 256
NF = 16
NBLK = 128
ROWS = 32768


def draw_freq_bins(key, part):
    key = jax.random.fold_in(key, 11)
    middle = 2 + jax.random.permutation(key, NFFT // 2 - 3)[:NF - 2]
    ends = jnp.array([1, NFFT // 2 - 1], dtype=jnp.int32)
    return jnp.concatenate([ends, middle.astype(jnp.int32)]).astype(jnp.int32)


def draw_volumes(key, part):
    key = jax.random.fold_in(key, 23)
    position = (jnp.arange(ROWS, dtype=jnp.float32) + 0.5) / ROWS
    radial = 0.25 + 0.75 * position
    spread = jnp.exp(jax.random.uniform(key, (ROWS,), jnp.float32, -1.2, 1.2))
    return (radial * spread).astype(jnp.float32)


def block_scale(rng, extent, split, smallest, largest):
    def one(dim, blocks):
        draws = jax.random.uniform(jax.random.fold_in(jax.random.fold_in(rng, 6), dim), (blocks,), jnp.float32, smallest / len(split), largest / len(split))
        return jnp.repeat(jnp.exp(draws), extent[dim] // blocks).reshape((-1,) + (1,) * (len(extent) - dim - 1))

    loudness = one(*split[0])
    for cut in split[1:]:
        loudness = loudness * one(*cut)
    return loudness


def gaussian(key, dims, width, most, shards=(), kind=jnp.bfloat16):
    values = jax.random.normal(key, dims, jnp.float32) * width
    if len(shards) > 0:
        values = block_scale(key, dims, shards, -0.22, 0.18) * values
    return jnp.clip(values, min=-most, max=most).astype(kind)


def setup_inputs(seed: int = 0) -> dict:
    splits = jax.random.split(jax.random.key(seed), 4)
    return {
        "segments": gaussian(splits[0], (NBLK, NFFT, ROWS), 1.0, 6.0, ((0, 4), (2, 32))),
        "volumes": draw_volumes(jax.random.fold_in(splits[3], 71), 0),
        "freq_bins": draw_freq_bins(jax.random.fold_in(splits[3], 71), 0),
    }


def make_table(freq_bins, fft_len):
    steps_t = jnp.arange(fft_len, dtype=jnp.int32)
    phase = freq_bins.astype(jnp.int32)[:, None] * steps_t[None, :] % fft_len
    angle = 2.0 * math.pi / fft_len * phase.astype(jnp.float32)
    window = 0.5 - 0.5 * jnp.cos(2.0 * math.pi / fft_len * steps_t.astype(jnp.float32))
    scale = window / math.sqrt(fft_len)
    return jnp.stack([scale * jnp.cos(angle), -scale * jnp.sin(angle)]).astype(jnp.bfloat16)

def reference(segments, volumes, freq_bins):
    dft_table = make_table(freq_bins, NFFT).reshape(2 * NF, NFFT)

    def one_segment(segment):
        return jnp.dot(dft_table.astype(jnp.float32), segment.astype(jnp.float32), preferred_element_type=jnp.float32)
    coefficients = lax.map(one_segment, segments)
    coefficients = coefficients.reshape(NBLK, 2, NF, ROWS)
    matrix = jnp.transpose(coefficients, (2, 3, 1, 0)).reshape(NF, ROWS, 2 * NBLK)
    root_rows = math.sqrt(ROWS)

    def one_frequency(columns):
        weighted = columns * volumes[:, None]
        gram = jnp.dot(columns.T, weighted, precision=lax.Precision.HIGHEST)
        lower_tri = jnp.linalg.cholesky(gram)
        basis_t = jax.scipy.linalg.solve_triangular(lower_tri, columns.T, lower=True)
        return (basis_t.T * root_rows, lower_tri.T / root_rows)
    modes, triangle = lax.map(one_frequency, matrix)
    return (modes, triangle)
```

```python
import functools
import math

import jax
import jax.numpy as jnp
from jax import lax
from jax.experimental import pallas as pl
from jax.experimental.pallas import tpu as pltpu
from jax.sharding import PartitionSpec as P

HIGHEST = lax.Precision.HIGHEST
HOPS = (0, 1, 3, 2)
GROUPS = ((0, 1), (2,), (3,))
PANEL = 32


def dot(a, b, dims, precision=None):
    return lax.dot_general(
        a, b, (dims, ((), ())), precision=precision, preferred_element_type=jnp.float32
    )


def dot3(a, b, dims):
    ah, bh = a.astype(jnp.bfloat16), b.astype(jnp.bfloat16)
    al = (a - ah.astype(jnp.float32)).astype(jnp.bfloat16)
    bl = (b - bh.astype(jnp.float32)).astype(jnp.bfloat16)
    return dot(ah, bh, dims) + (dot(ah, bl, dims) + dot(al, bh, dims))


def transform_kernel(bins_ref, seg_ref, *refs):
    outs, (table, landing) = refs[:-2], refs[-2:]
    group, fft_len = seg_ref.shape[0], seg_ref.shape[1]
    n_rows = table.shape[0]
    per_hop = n_rows // len(HOPS)
    n_local = per_hop // 2

    @pl.when((pl.program_id(0) == 0) & (pl.program_id(1) == 0))
    def _():
        me = lax.axis_index("freq")
        row = lax.broadcasted_iota(jnp.int32, (n_rows, fft_len), 0)
        step = lax.broadcasted_iota(jnp.int32, (n_rows, fft_len), 1)
        bins = jnp.zeros((n_rows, fft_len), jnp.int32)
        for h, hop in enumerate(HOPS):
            home = lax.rem(me + hop, len(HOPS))
            for j in range(n_local):
                which = bins_ref[home * n_local + j]
                bins = jnp.where(row // 2 == h * n_local + j, which, bins)
        phase = lax.rem(bins * step, fft_len)
        angle = 2.0 * math.pi / fft_len * phase.astype(jnp.float32)
        window = 0.5 - 0.5 * jnp.cos(2.0 * math.pi / fft_len * step.astype(jnp.float32))
        scale = window / math.sqrt(fft_len)
        wave = jnp.where(lax.rem(row, 2) == 0, jnp.cos(angle), -jnp.sin(angle))
        table[...] = (scale * wave).astype(jnp.bfloat16)

    for b in range(group):
        sums = dot(table[...], seg_ref[b], ((1,), (0,)))
        for k in range(landing.shape[0]):
            tile = slice(128 * k, 128 * k + 128)
            landing[k, pl.ds(b, n_rows, stride=group), :] = sums[:, tile]
    n = 0
    for js in GROUPS:
        for h in range(len(HOPS)):
            out = outs[n]
            n += 1
            for i, j in enumerate(js):
                for c in range(2):
                    r = (h * per_hop + j * 2 + c) * group
                    for k in range(landing.shape[0]):
                        tile = slice(128 * k, 128 * k + 128)
                        out[i, c, :, tile] = landing[k, r : r + group, :]


def transform(bins, segments):
    n_seg, fft_len, n_x = segments.shape
    group, cols = 8, n_x // 2
    n_rows = 2 * bins.shape[0]
    shapes, specs = [], []
    for js in GROUPS:
        for _ in HOPS:
            shapes.append(jax.ShapeDtypeStruct((len(js), 2, n_seg, n_x), jnp.float32))
            specs.append(
                pl.BlockSpec((len(js), 2, group, cols), lambda g, x: (0, 0, g, x))
            )
    outs = pl.pallas_call(
        transform_kernel,
        out_shape=shapes,
        grid=(n_seg // group, n_x // cols),
        in_specs=[
            pl.BlockSpec(memory_space=pltpu.SMEM),
            pl.BlockSpec((group, fft_len, cols), lambda g, x: (g, 0, x)),
        ],
        out_specs=specs,
        scratch_shapes=[
            pltpu.VMEM((n_rows, fft_len), jnp.bfloat16),
            pltpu.VMEM((cols // 128, n_rows * group, 128), jnp.float32),
        ],
        compiler_params=pltpu.CompilerParams(vmem_limit_bytes=40 << 20),
        cost_estimate=pl.CostEstimate(
            flops=2 * n_seg * fft_len * n_x * n_rows,
            bytes_accessed=20 << 20,
            transcendentals=0,
        ),
    )(bins, segments)
    k = len(HOPS)
    return [outs[i * k : (i + 1) * k] for i in range(len(GROUPS))]


def gram_kernel(halves, vol_ref, *refs):
    pieces, (mt_ref, mine_ref, other_ref, total) = refs[:4], refs[4:]
    me, core = lax.axis_index("freq"), lax.rem(lax.axis_index("space"), 2)
    n_seg = pieces[0].shape[2]
    n_all = n_seg * len(HOPS)
    for h, hop in enumerate(HOPS):
        source = lax.rem(me + len(HOPS) - hop, len(HOPS))
        for c in range(2):
            start = pl.multiple_of(c * n_all + source * n_seg, n_seg)
            mt_ref[0, pl.ds(start, n_seg), :] = pieces[h][0, c]
    m = mt_ref[0]
    g = dot3(m, m * vol_ref[...], ((1,), (1,)))
    n = m.shape[0] // 2
    blocks = (g[:n, :n], g[n:, :n], g[n:, n:])
    if halves:
        for i, block in enumerate(blocks):
            total[i] = block
        k = n // 2
        mine_ref[...] = total[:, pl.ds(pl.multiple_of(core * k, k), k), :]
        other_ref[...] = total[:, pl.ds(pl.multiple_of((1 - core) * k, k), k), :]
    else:

        @pl.when(pl.program_id(0) == core)
        def _():
            for i, block in enumerate(blocks):
                mine_ref[i] = block

        @pl.when(pl.program_id(0) != core)
        def _():
            for i, block in enumerate(blocks):
                other_ref[i] = block


def gram(volumes, pieces):
    nj, two, n_seg, n_x = pieces[0].shape
    n = two * n_seg * len(HOPS)
    halves = nj == 1
    part = (3, n // 4 if halves else n // 2, n // 2)
    piece = pl.BlockSpec((1, two, n_seg, n_x), lambda j: (j, 0, 0, 0))
    whole = pl.BlockSpec(part, lambda j: (0, 0, 0))
    return pl.pallas_call(
        functools.partial(gram_kernel, halves),
        out_shape=[
            jax.ShapeDtypeStruct((nj, n, n_x), jnp.float32),
            jax.ShapeDtypeStruct(part, jnp.float32),
            jax.ShapeDtypeStruct(part, jnp.float32),
        ],
        grid=(nj,),
        in_specs=[pl.BlockSpec((1, n_x), lambda j: (0, 0))] + [piece] * len(HOPS),
        out_specs=[pl.BlockSpec((1, n, n_x), lambda j: (j, 0, 0)), whole, whole],
        scratch_shapes=[pltpu.VMEM((3, n // 2, n // 2), jnp.float32)],
        compiler_params=pltpu.CompilerParams(vmem_limit_bytes=40 << 20),
        cost_estimate=pl.CostEstimate(
            flops=6 * nj * n * n * n_x,
            bytes_accessed=8 * nj * n * n_x,
            transcendentals=0,
        ),
    )(volumes.reshape(1, n_x), *pieces)


def space_pairs(kind):
    pairs = []
    for i in range(32):
        y, x, core = i // 8, i // 2 % 4, i % 2
        if kind == "core":
            core = 1 - core
        else:
            along_x = (kind < 2) == (core == 0)
            flip = (lambda v: v ^ 1) if kind % 2 == 0 else (lambda v: 3 - v)
            x, y = (flip(x), y) if along_x else (x, flip(y))
        pairs.append((i, (y * 4 + x) * 2 + core))
    return pairs


def swap(value, kind):
    return lax.ppermute(value, "space", space_pairs(kind))


def sum_over_space(mine, other):
    value = mine + swap(other, "core")
    for kind in range(4):
        value = value + swap(value, kind)
    return value


def factor(work):
    n = work.shape[0]
    rows = lax.broadcasted_iota(jnp.int32, (8, 128), 0)
    n_sub, half = PANEL // 8, n // 128
    for base in range(0, n, PANEL):
        tile, lane = base // 128, base % 128
        tiles = [
            t for t in range(2 * half)
            if (tile <= t < half) or (t >= half and (t - half) * 128 < base + PANEL)
        ]
        live = [
            {t: work[base + 8 * i : base + 8 * i + 8, 128 * t : 128 * t + 128] for t in tiles}
            for i in range(n_sub)
        ]
        done = [{} for _ in range(n_sub)]
        column = [
            {
                j: jnp.broadcast_to(live[i][tile][:, lane + j : lane + j + 1], (8, 128))
                for j in range(8 * i + 8)
            }
            for i in range(n_sub)
        ]
        for p in range(PANEL):
            ip, sp = p // 8, p % 8
            pivot = jnp.broadcast_to(column[ip][p][sp : sp + 1, :], (8, 128))
            root = lax.rsqrt(pivot)
            inv = root * root
            mult = {i: column[i][p] * inv for i in range(ip, n_sub)}
            for j in range(p + 1, PANEL):
                ij = j // 8
                entry = jnp.broadcast_to(column[ij][p][j % 8 : j % 8 + 1, :], (8, 128))
                for i in range(ij, n_sub):
                    column[i][j] = column[i][j] - mult[i] * entry
            for t in tiles:
                row = jnp.broadcast_to(live[ip][t][sp : sp + 1, :], (8, 128))
                scaled = row * root
                done[ip][t] = scaled if sp == 0 else jnp.where(rows == sp, scaled, done[ip][t])
                for i in range(ip, n_sub):
                    if i > ip or sp < 7:
                        live[i][t] = live[i][t] - mult[i] * row
        for i in range(n_sub):
            for t in tiles:
                work[base + 8 * i : base + 8 * i + 8, 128 * t : 128 * t + 128] = done[i][t]
        after = base + PANEL
        first = after // 128
        for blk in range(first, half):
            lo, hi = max(after, 128 * blk), 128 * blk + 128
            left = work[base:after, 128 * blk : hi]
            for c0, c1 in ((128 * first, n), (n, n + (after + 127) // 128 * 128)):
                right = work[base:after, c0:c1]
                update = dot(left, right, ((0,), (0,)), HIGHEST)
                work[lo:hi, c0:c1] = work[lo:hi, c0:c1] - update[lo - 128 * blk :, :]


def load_gram(work, g11, g21, g22):
    n = work.shape[0]
    h = n // 2
    work[:h, :h] = g11
    work[:h, h:n] = g21.T
    work[h:, h:n] = g22
    work[h:, :h] = g21
    r = lax.broadcasted_iota(jnp.int32, (n, n), 0)
    c = lax.broadcasted_iota(jnp.int32, (n, n), 1)
    work[:, n:] = jnp.where(r == c, 1.0, 0.0)


def masked_factors(work):
    n = work.shape[0]
    r = lax.broadcasted_iota(jnp.int32, (n, n), 0)
    c = lax.broadcasted_iota(jnp.int32, (n, n), 1)
    upper = jnp.where(r <= c, work[:, :n], 0.0)
    inverse = jnp.where(r >= c, work[:, n:], 0.0)
    return upper, inverse


def factor_kernel(g_ref, out_ref, work):
    load_gram(work, g_ref[0], g_ref[1], g_ref[2])
    factor(work)
    upper, inverse = masked_factors(work)
    out_ref[0] = upper
    out_ref[1] = inverse


def factor_call(blocks):
    n = 2 * blocks.shape[2]
    return pl.pallas_call(
        factor_kernel,
        out_shape=jax.ShapeDtypeStruct((2, n, n), jnp.float32),
        scratch_shapes=[pltpu.VMEM((n, 2 * n), jnp.float32)],
        compiler_params=pltpu.CompilerParams(vmem_limit_bytes=40 << 20),
        cost_estimate=pl.CostEstimate(
            flops=16 * n * n * n, bytes_accessed=12 * n * n, transcendentals=0
        ),
    )(blocks)


def modes_pair_kernel(root_rows, mine_ref, other_ref, mt_ref, *refs):
    modes_ref, tri_ref = refs[-2:]
    core = lax.rem(lax.axis_index("space"), 2)
    is_mine = pl.program_id(0) == core

    def emit(src):
        modes_ref[0] = dot(mt_ref[0], src[1] * root_rows, ((0,), (1,)), HIGHEST)
        tri_ref[0] = src[0] * (1.0 / root_rows)

    @pl.when(is_mine)
    def _():
        emit(mine_ref)

    @pl.when(jnp.logical_not(is_mine))
    def _():
        emit(other_ref)


def modes_one_kernel(root_rows, mine_ref, other_ref, mt_ref, *refs):
    modes_ref, tri_ref, work, g = refs[-4:]

    @pl.when(pl.program_id(0) == 0)
    def _():
        core = lax.rem(lax.axis_index("space"), 2)
        k = mine_ref.shape[1]
        g[:, pl.ds(pl.multiple_of(core * k, k), k), :] = mine_ref[...]
        g[:, pl.ds(pl.multiple_of((1 - core) * k, k), k), :] = other_ref[...]
        load_gram(work, g[0], g[1], g[2])
        factor(work)
        upper, inverse = masked_factors(work)
        n = work.shape[0]
        tri_ref[0] = upper * (1.0 / root_rows)
        work[:, n:] = inverse * root_rows

    n = work.shape[0]
    modes_ref[0] = dot(mt_ref[0], work[:, n:], ((0,), (1,)), HIGHEST)


def modes_call(js, n_local, root_rows, mine, other, mt, before):
    nj, n, n_x = mt.shape
    shapes = [
        jax.ShapeDtypeStruct((n_local, n_x, n), jnp.float32),
        jax.ShapeDtypeStruct((n_local, n, n), jnp.float32),
    ]
    whole = pl.BlockSpec(mine.shape, lambda j: (0,) * mine.ndim)
    first = js[0]
    if nj == 1:
        parts = 4
        body, scratch = modes_one_kernel, [
            pltpu.VMEM((n, 2 * n), jnp.float32),
            pltpu.VMEM((3, n // 2, n // 2), jnp.float32),
        ]
        grid = (parts,)
        mt_spec = pl.BlockSpec((1, n, n_x // parts), lambda x: (0, 0, x))
        out_specs = [
            pl.BlockSpec((1, n_x // parts, n), lambda x: (first, x, 0)),
            pl.BlockSpec((1, n, n), lambda x: (first, 0, 0)),
        ]
    else:
        body, scratch = modes_pair_kernel, []
        grid = (nj,)
        mt_spec = pl.BlockSpec((1, n, n_x), lambda j: (j, 0, 0))
        out_specs = [
            pl.BlockSpec((1, n_x, n), lambda j: (first + j, 0, 0)),
            pl.BlockSpec((1, n, n), lambda j: (first + j, 0, 0)),
        ]
    before = list(before)
    return pl.pallas_call(
        functools.partial(body, root_rows),
        out_shape=shapes,
        grid=grid,
        in_specs=[whole, whole, mt_spec] + [pl.BlockSpec(memory_space=pl.ANY)] * len(before),
        out_specs=out_specs,
        scratch_shapes=scratch,
        input_output_aliases={3 + i: i for i in range(len(before))},
        compiler_params=pltpu.CompilerParams(vmem_limit_bytes=40 << 20),
        cost_estimate=pl.CostEstimate(
            flops=12 * nj * n * n * n_x,
            bytes_accessed=8 * nj * n * n_x,
            transcendentals=0,
        ),
    )(mine, other, mt, *before)


def on_device(segments, volumes, freq_bins):
    n_freq = lax.axis_size("freq")
    n_local = freq_bins.shape[0] // n_freq
    root_rows = math.sqrt(segments.shape[2] * lax.axis_size("space"))
    sent = transform(freq_bins, segments)
    outs = ()
    previous = None
    arrived = []
    for js, pieces in zip(GROUPS, sent):
        got = [pieces[0]]
        for h, hop in enumerate(HOPS):
            if hop == 0:
                continue
            piece = pieces[h]
            if previous is not None:
                piece, previous[h] = lax.optimization_barrier((piece, previous[h]))
            got.append(lax.ppermute(piece, "freq", [(i, (i + hop) % n_freq) for i in range(n_freq)]))
        if previous is not None:
            arrived[-1] = previous
        previous = list(got)
        arrived.append(previous)
    grams = [gram(volumes, got) for got in arrived]
    for js, (mt, mine, other) in zip(GROUPS, grams):
        value = sum_over_space(mine, other)
        if len(js) == 2:
            value = factor_call(value)
        outs = modes_call(js, n_local, root_rows, value, swap(value, "core"), mt, outs)
    return tuple(outs)


def solution(mesh):
    placed = (P("freq", None, "space"), P("space"), P())
    return jax.shard_map(
        on_device,
        mesh=mesh,
        in_specs=placed,
        out_specs=(P("freq", "space", None), P("freq", None, None)),
        check_vma=False,
    )
```

```python
import functools
import math

import jax
import jax.numpy as jnp
from jax import lax
from jax.experimental import pallas as pl
from jax.experimental.pallas import tpu as pltpu
from jax.sharding import PartitionSpec as P

HIGHEST = lax.Precision.HIGHEST
HOPS = (0, 1, 3, 2)
GROUPS = ((0, 1), (2, 3))
PANEL = 32
CUTS = (4,)
STEPS = (0, 1, 2, 3)
EARLY = 2
IN_VMEM = pl.BlockSpec(memory_space=pltpu.VMEM)
IN_HBM = pl.BlockSpec(memory_space=pltpu.HBM)
SMALL = pl.CostEstimate(flops=1000, bytes_accessed=1000, transcendentals=0)


def dot(a, b, dims, precision=None):
    return lax.dot_general(
        a, b, (dims, ((), ())), precision=precision, preferred_element_type=jnp.float32
    )


def dot3(a, b, dims):
    ah, bh = a.astype(jnp.bfloat16), b.astype(jnp.bfloat16)
    al = (a - ah.astype(jnp.float32)).astype(jnp.bfloat16)
    bl = (b - bh.astype(jnp.float32)).astype(jnp.bfloat16)
    return dot(ah, bh, dims) + (dot(ah, bl, dims) + dot(al, bh, dims))


def transform_kernel(bins_in, seg_ref, *refs):
    outs, (table, landing, held, sems, bins_ref, bins_sem) = refs[:-6], refs[-6:]
    n_seg, fft_len = seg_ref.shape[0], seg_ref.shape[1]
    group, n_rows = 8, table.shape[0]
    per_hop = n_rows // len(HOPS)
    n_local = per_hop // 2

    batch = 4

    def segment_copy(b):
        some = pl.ds(b * batch, batch)
        return pltpu.make_async_copy(seg_ref.at[some], held.at[some], sems.at[b])

    bins_copy = pltpu.make_async_copy(bins_in, bins_ref, bins_sem)
    bins_copy.start()
    for b in range(n_seg // batch):
        segment_copy(b).start()
    me = lax.axis_index("freq")
    row = lax.broadcasted_iota(jnp.int32, (n_rows, fft_len), 0)
    step = lax.broadcasted_iota(jnp.int32, (n_rows, fft_len), 1)
    bins = jnp.zeros((n_rows, fft_len), jnp.int32)
    bins_copy.wait()
    for h, hop in enumerate(HOPS):
        home = lax.rem(me + hop, len(HOPS))
        for j in range(n_local):
            which = bins_ref[home * n_local + j]
            bins = jnp.where(row // 2 == h * n_local + j, which, bins)
    phase = lax.rem(bins * step, fft_len)
    angle = 2.0 * math.pi / fft_len * phase.astype(jnp.float32)
    window = 0.5 - 0.5 * jnp.cos(2.0 * math.pi / fft_len * step.astype(jnp.float32))
    scale = window / math.sqrt(fft_len)
    wave = jnp.where(lax.rem(row, 2) == 0, jnp.cos(angle), -jnp.sin(angle))
    table[...] = (scale * wave).astype(jnp.bfloat16)

    @pl.loop(0, n_seg // group)
    def _(g):
        base = pl.multiple_of(g * group, group)
        for b in range(group):
            if b % batch == 0:
                segment_copy(g * (group // batch) + b // batch).wait()
            sums = dot(table[...], held[base + b], ((1,), (0,)))
            for k in range(landing.shape[0]):
                tile = slice(128 * k, 128 * k + 128)
                landing[k, pl.ds(b, n_rows, stride=group), :] = sums[:, tile]
        n = 0
        for js in GROUPS:
            for h in range(len(HOPS)):
                for i, j in enumerate(js):
                    for c in range(2):
                        r = (h * per_hop + j * 2 + c) * group
                        for k in range(landing.shape[0]):
                            tile = slice(128 * k, 128 * k + 128)
                            outs[n][i, c, pl.ds(base, group), tile] = landing[k, r : r + group, :]
                n += 1


def transform(bins, segments):
    n_seg, fft_len, n_x = segments.shape
    n_rows = 2 * bins.shape[0]
    shapes = [
        jax.ShapeDtypeStruct((len(js), 2, n_seg, n_x), jnp.float32)
        for js in GROUPS
        for _ in HOPS
    ]
    outs = pl.pallas_call(
        transform_kernel,
        out_shape=shapes,
        in_specs=[IN_HBM, IN_HBM],
        out_specs=[IN_VMEM] * len(shapes),
        scratch_shapes=[
            pltpu.VMEM((n_rows, fft_len), jnp.bfloat16),
            pltpu.VMEM((n_x // 128, n_rows * 8, 128), jnp.float32),
            pltpu.VMEM(segments.shape, segments.dtype),
            pltpu.SemaphoreType.DMA((n_seg,)),
            pltpu.SMEM(bins.shape, bins.dtype),
            pltpu.SemaphoreType.DMA,
        ],
        compiler_params=pltpu.CompilerParams(vmem_limit_bytes=50 << 20),
        cost_estimate=SMALL,
    )(bins, segments)
    k = len(HOPS)
    return [outs[i * k : (i + 1) * k] for i in range(len(GROUPS))]


def gram_kernel(vol_ref, *refs):
    pieces, (mt_ref, mine_ref, other_ref, packed) = refs[:4], refs[4:]
    me, core = lax.axis_index("freq"), lax.rem(lax.axis_index("space"), 2)
    n_seg = pieces[0].shape[2]
    n_all = n_seg * len(HOPS)
    row = lax.broadcasted_iota(jnp.int32, (n_all, n_all), 0)
    col = lax.broadcasted_iota(jnp.int32, (n_all, n_all), 1)
    for j in range(mt_ref.shape[0]):
        for h, hop in enumerate(HOPS):
            source = lax.rem(me + len(HOPS) - hop, len(HOPS))
            for c in range(2):
                start = pl.multiple_of(c * n_all + source * n_seg, n_seg)
                mt_ref[j, pl.ds(start, n_seg), :] = pieces[h][j, c]
        m = mt_ref[j]
        g = dot3(m, m * vol_ref[...], ((1,), (1,)))
        g11, g21, g22 = g[:n_all, :n_all], g[n_all:, :n_all], g[n_all:, n_all:]
        packed[j, :n_all, :] = g21
        packed[j, n_all : 2 * n_all, :] = jnp.where(row >= col, g11, g22)
        diagonal = jnp.sum(jnp.where(row == col, g22, 0.0), axis=0, keepdims=True)
        packed[j, 2 * n_all :, :] = jnp.broadcast_to(diagonal, (8, n_all))
    mine_ref[...] = packed[core]
    other_ref[...] = packed[1 - core]


def gram(volumes, pieces):
    nj, two, n_seg, n_x = pieces[0].shape
    n = two * n_seg * len(HOPS)
    part = (n + 8, n // 2)
    return pl.pallas_call(
        gram_kernel,
        out_shape=[
            jax.ShapeDtypeStruct((nj, n, n_x), jnp.float32),
            jax.ShapeDtypeStruct(part, jnp.float32),
            jax.ShapeDtypeStruct(part, jnp.float32),
        ],
        in_specs=[IN_VMEM] * (1 + len(HOPS)),
        out_specs=[IN_VMEM] * 3,
        scratch_shapes=[pltpu.VMEM((nj,) + part, jnp.float32)],
        compiler_params=pltpu.CompilerParams(vmem_limit_bytes=16 << 20),
        cost_estimate=SMALL,
    )(volumes.reshape(1, n_x), *pieces)


def space_pairs(kind):
    pairs = []
    for i in range(32):
        y, x, core = i // 8, i // 2 % 4, i % 2
        if kind == "core":
            core = 1 - core
        else:
            along_x = (kind < 2) == (core == 0)
            flip = (lambda v: v ^ 1) if kind % 2 == 0 else (lambda v: 3 - v)
            x, y = (flip(x), y) if along_x else (x, flip(y))
        pairs.append((i, (y * 4 + x) * 2 + core))
    return pairs


def swap(value, kind):
    return lax.ppermute(value, "space", space_pairs(kind))


def add_steps(value, steps):
    for kind in steps:
        value = value + swap(value, kind)
    return value


def factor(work, begin, end):
    n = work.shape[0]
    rows = lax.broadcasted_iota(jnp.int32, (8, 128), 0)
    n_sub, half = PANEL // 8, n // 128
    for base in range(begin * PANEL, end * PANEL, PANEL):
        tile, lane = base // 128, base % 128
        tiles = [
            t for t in range(2 * half)
            if (tile <= t < half) or (t >= half and (t - half) * 128 < base + PANEL)
        ]
        live = [
            {t: work[base + 8 * i : base + 8 * i + 8, 128 * t : 128 * t + 128] for t in tiles}
            for i in range(n_sub)
        ]
        done = [{} for _ in range(n_sub)]
        column = [
            {
                j: jnp.broadcast_to(live[i][tile][:, lane + j : lane + j + 1], (8, 128))
                for j in range(8 * i + 8)
            }
            for i in range(n_sub)
        ]
        for p in range(PANEL):
            ip, sp = p // 8, p % 8
            pivot = jnp.broadcast_to(column[ip][p][sp : sp + 1, :], (8, 128))
            root = lax.rsqrt(pivot)
            inv = root * root
            mult = {i: column[i][p] * inv for i in range(ip, n_sub)}
            for j in range(p + 1, PANEL):
                ij = j // 8
                entry = jnp.broadcast_to(column[ij][p][j % 8 : j % 8 + 1, :], (8, 128))
                for i in range(ij, n_sub):
                    column[i][j] = column[i][j] - mult[i] * entry
            for t in tiles:
                row = jnp.broadcast_to(live[ip][t][sp : sp + 1, :], (8, 128))
                scaled = row * root
                done[ip][t] = scaled if sp == 0 else jnp.where(rows == sp, scaled, done[ip][t])
                for i in range(ip, n_sub):
                    if i > ip or sp < 7:
                        live[i][t] = live[i][t] - mult[i] * row
        for i in range(n_sub):
            for t in tiles:
                work[base + 8 * i : base + 8 * i + 8, 128 * t : 128 * t + 128] = done[i][t]
        after = base + PANEL
        first = after // 128
        for blk in range(first, half):
            lo, hi = max(after, 128 * blk), 128 * blk + 128
            left = work[base:after, 128 * blk : hi]
            for c0, c1 in ((128 * first, n), (n, n + (after + 127) // 128 * 128)):
                right = work[base:after, c0:c1]
                update = dot(left, right, ((0,), (0,)), HIGHEST)
                work[lo:hi, c0:c1] = work[lo:hi, c0:c1] - update[lo - 128 * blk :, :]


def load_gram(work, packed):
    n = work.shape[0]
    h = n // 2
    row = lax.broadcasted_iota(jnp.int32, (h, h), 0)
    col = lax.broadcasted_iota(jnp.int32, (h, h), 1)
    g21, square = packed[:h, :], packed[h:n, :]
    turned = square.T
    work[:h, :h] = jnp.where(row >= col, square, turned)
    work[:h, h:n] = g21.T
    work[h:, :h] = g21
    g22 = jnp.where(row < col, square, turned)
    work[h:, h:n] = jnp.where(row == col, packed[n : n + 1, :], g22)
    row = lax.broadcasted_iota(jnp.int32, (n, n), 0)
    col = lax.broadcasted_iota(jnp.int32, (n, n), 1)
    work[:, n:] = jnp.where(row == col, 1.0, 0.0)


def factor_kernel(begin, end, in_ref, out_ref, work):
    n = work.shape[0]
    if begin == 0:
        load_gram(work, in_ref)
    else:
        work[...] = in_ref[...]
    factor(work, begin, end)
    if end * PANEL < n:
        out_ref[...] = work[...]
    else:
        row = lax.broadcasted_iota(jnp.int32, (n, n), 0)
        col = lax.broadcasted_iota(jnp.int32, (n, n), 1)
        out_ref[0] = jnp.where(row <= col, work[:, :n], 0.0)
        out_ref[1] = jnp.where(row >= col, work[:, n:], 0.0)


def factor_call(value, cuts):
    n = 2 * value.shape[1]
    ends = tuple(cuts) + (n // PANEL,)
    for begin, end in zip((0,) + ends, ends):
        last = end * PANEL == n
        value = pl.pallas_call(
            functools.partial(factor_kernel, begin, end),
            out_shape=jax.ShapeDtypeStruct((2, n, n) if last else (n, 2 * n), jnp.float32),
            in_specs=[IN_VMEM],
            out_specs=IN_VMEM,
            scratch_shapes=[pltpu.VMEM((n, 2 * n), jnp.float32)],
            compiler_params=pltpu.CompilerParams(vmem_limit_bytes=8 << 20),
            cost_estimate=pl.CostEstimate(
                flops=(end - begin) << 29, bytes_accessed=1000, transcendentals=0
            ),
        )(value)
    return value


def modes_kernel(js, root_rows, mine_ref, other_ref, mt_ref, *refs):
    modes_ref, tri_ref, inverse, held, tri, sems, tri_sems = refs[-7:]
    core = lax.rem(lax.axis_index("space"), 2)
    n_parts, part = held.shape[1], held.shape[2]

    def tri_copy(i):
        return pltpu.make_async_copy(tri.at[i], tri_ref.at[js[i]], tri_sems.at[i])

    def modes_copy(i, q):
        rows = pl.ds(q * part, part)
        return pltpu.make_async_copy(held.at[i, q], modes_ref.at[js[i], rows, :], sems.at[i, q])

    for i in range(len(js)):

        @pl.when(core == i)
        def _():
            tri[i] = mine_ref[0] * (1.0 / root_rows)
            inverse[i] = mine_ref[1] * root_rows

        @pl.when(core != i)
        def _():
            tri[i] = other_ref[0] * (1.0 / root_rows)
            inverse[i] = other_ref[1] * root_rows

        tri_copy(i).start()
    for i in range(len(js)):
        for q in range(n_parts):
            rows = slice(q * part, q * part + part)
            held[i, q] = dot3(mt_ref[i, :, rows], inverse[i], ((0,), (1,)))
            modes_copy(i, q).start()
    for i in range(len(js)):
        tri_copy(i).wait()
        for q in range(n_parts):
            modes_copy(i, q).wait()


def modes_call(js, n_local, root_rows, mine, other, mt, before):
    nj, n, n_x = mt.shape
    parts = 4
    before = list(before)
    return pl.pallas_call(
        functools.partial(modes_kernel, js, root_rows),
        out_shape=[
            jax.ShapeDtypeStruct((n_local, n_x, n), jnp.float32),
            jax.ShapeDtypeStruct((n_local, n, n), jnp.float32),
        ],
        in_specs=[IN_VMEM] * 3 + [IN_HBM] * len(before),
        out_specs=[IN_HBM, IN_HBM],
        scratch_shapes=[
            pltpu.VMEM((nj, n, n), jnp.float32),
            pltpu.VMEM((nj, parts, n_x // parts, n), jnp.float32),
            pltpu.VMEM((nj, n, n), jnp.float32),
            pltpu.SemaphoreType.DMA((nj, parts)),
            pltpu.SemaphoreType.DMA((nj,)),
        ],
        input_output_aliases={3 + i: i for i in range(len(before))},
        compiler_params=pltpu.CompilerParams(vmem_limit_bytes=16 << 20),
        cost_estimate=SMALL,
    )(mine, other, mt, *before)


def on_device(segments, volumes, freq_bins):
    n_freq = lax.axis_size("freq")
    n_local = freq_bins.shape[0] // n_freq
    root_rows = math.sqrt(segments.shape[2] * lax.axis_size("space"))
    sent = transform(freq_bins, segments)
    arrived = []
    for pieces in sent:
        got = [pieces[0]]
        for h, hop in enumerate(HOPS):
            if hop == 0:
                continue
            piece = pieces[h]
            if arrived:
                piece, arrived[-1][h] = lax.optimization_barrier((piece, arrived[-1][h]))
            got.append(lax.ppermute(piece, "freq", [(i, (i + hop) % n_freq) for i in range(n_freq)]))
        arrived.append(got)
    sums = []
    for got in arrived:
        mt, mine, other = gram(volumes, got)
        value = add_steps(mine + swap(other, "core"), STEPS[:EARLY])
        value, volumes = lax.optimization_barrier((value, volumes))
        sums.append((mt, value))
    outs = ()
    for js, (mt, value) in zip(GROUPS, sums):
        value = factor_call(add_steps(value, STEPS[EARLY:]), CUTS if js[0] == 0 else ())
        outs = modes_call(js, n_local, root_rows, value, swap(value, "core"), mt, outs)
    return tuple(outs)


def solution(mesh):
    placed = (P("freq", None, "space"), P("space"), P())
    return jax.shard_map(
        on_device,
        mesh=mesh,
        in_specs=placed,
        out_specs=(P("freq", "space", None), P("freq", None, None)),
        check_vma=False,
    )
```

```python
import functools
import math

import jax
import jax.numpy as jnp
from jax import lax
from jax.experimental import pallas as pl
from jax.experimental.pallas import tpu as pltpu
from jax.sharding import PartitionSpec as P

HIGHEST = lax.Precision.HIGHEST
HOPS = (0, 2, 1, 3)
GROUPS = ((0, 1), (2, 3))
PANEL = 32
PAIRS = ((0, 0), (0, 1), (1, 0), (0, 2), (2, 0), (1, 1))
CUTS = (4,)
IN_VMEM = pl.BlockSpec(memory_space=pltpu.VMEM)
IN_HBM = pl.BlockSpec(memory_space=pltpu.HBM)
SMALL = pl.CostEstimate(flops=1000, bytes_accessed=1000, transcendentals=0)


def dot(a, b, dims, precision=None):
    return lax.dot_general(
        a, b, (dims, ((), ())), precision=precision, preferred_element_type=jnp.float32
    )


def dot3(a, b, dims):
    ah, bh = a.astype(jnp.bfloat16), b.astype(jnp.bfloat16)
    al = (a - ah.astype(jnp.float32)).astype(jnp.bfloat16)
    bl = (b - bh.astype(jnp.float32)).astype(jnp.bfloat16)
    return dot(ah, bh, dims) + (dot(ah, bl, dims) + dot(al, bh, dims))


def transform_kernel(bins_in, seg_ref, *refs):
    outs, (table, landing, held, sems, bins_ref, bins_sem) = refs[:-6], refs[-6:]
    n_seg, fft_len = seg_ref.shape[0], seg_ref.shape[1]
    group, n_rows = 8, table.shape[0]
    per_hop = n_rows // len(HOPS)
    n_local = per_hop // 2

    batch = 4

    def segment_copy(b):
        some = pl.ds(b * batch, batch)
        return pltpu.make_async_copy(seg_ref.at[some], held.at[some], sems.at[b])

    bins_copy = pltpu.make_async_copy(bins_in, bins_ref, bins_sem)
    bins_copy.start()
    for b in range(n_seg // batch):
        segment_copy(b).start()
    me = lax.axis_index("freq")
    row = lax.broadcasted_iota(jnp.int32, (n_rows, fft_len), 0)
    step = lax.broadcasted_iota(jnp.int32, (n_rows, fft_len), 1)
    bins = jnp.zeros((n_rows, fft_len), jnp.int32)
    bins_copy.wait()
    for h, hop in enumerate(HOPS):
        home = lax.rem(me + hop, len(HOPS))
        for j in range(n_local):
            which = bins_ref[home * n_local + j]
            bins = jnp.where(row // 2 == h * n_local + j, which, bins)
    phase = lax.rem(bins * step, fft_len)
    angle = 2.0 * math.pi / fft_len * phase.astype(jnp.float32)
    window = 0.5 - 0.5 * jnp.cos(2.0 * math.pi / fft_len * step.astype(jnp.float32))
    scale = window / math.sqrt(fft_len)
    wave = jnp.where(lax.rem(row, 2) == 0, jnp.cos(angle), -jnp.sin(angle))
    table[...] = (scale * wave).astype(jnp.bfloat16)

    @pl.loop(0, n_seg // group)
    def _(g):
        base = pl.multiple_of(g * group, group)
        for b in range(group):
            if b % batch == 0:
                segment_copy(g * (group // batch) + b // batch).wait()
            sums = dot(table[...], held[base + b], ((1,), (0,)))
            for k in range(landing.shape[0]):
                tile = slice(128 * k, 128 * k + 128)
                landing[k, pl.ds(b, n_rows, stride=group), :] = sums[:, tile]
        n = 0
        for js in GROUPS:
            for h in range(len(HOPS)):
                for i, j in enumerate(js):
                    for c in range(2):
                        r = (h * per_hop + j * 2 + c) * group
                        for k in range(landing.shape[0]):
                            tile = slice(128 * k, 128 * k + 128)
                            outs[n][i, c, pl.ds(base, group), tile] = landing[k, r : r + group, :]
                n += 1


def transform(bins, segments):
    n_seg, fft_len, n_x = segments.shape
    n_rows = 2 * bins.shape[0]
    shapes = [
        jax.ShapeDtypeStruct((len(js), 2, n_seg, n_x), jnp.float32)
        for js in GROUPS
        for _ in HOPS
    ]
    outs = pl.pallas_call(
        transform_kernel,
        out_shape=shapes,
        in_specs=[IN_HBM, IN_HBM],
        out_specs=[IN_VMEM] * len(shapes),
        scratch_shapes=[
            pltpu.VMEM((n_rows, fft_len), jnp.bfloat16),
            pltpu.VMEM((n_x // 128, n_rows * 8, 128), jnp.float32),
            pltpu.VMEM(segments.shape, segments.dtype),
            pltpu.SemaphoreType.DMA((n_seg,)),
            pltpu.SMEM(bins.shape, bins.dtype),
            pltpu.SemaphoreType.DMA,
        ],
        compiler_params=pltpu.CompilerParams(vmem_limit_bytes=50 << 20),
        cost_estimate=SMALL,
    )(bins, segments)
    k = len(HOPS)
    return [outs[i * k : (i + 1) * k] for i in range(len(GROUPS))]


def gram_kernel(vol_ref, *refs):
    pieces, (mt_ref, mine_ref, other_ref, packed) = refs[:4], refs[4:]
    me, core = lax.axis_index("freq"), lax.rem(lax.axis_index("space"), 2)
    n_seg = pieces[0].shape[2]
    n_all = n_seg * len(HOPS)
    row = lax.broadcasted_iota(jnp.int32, (n_all, n_all), 0)
    col = lax.broadcasted_iota(jnp.int32, (n_all, n_all), 1)
    for j in range(mt_ref.shape[0]):
        for h, hop in enumerate(HOPS):
            source = lax.rem(me + len(HOPS) - hop, len(HOPS))
            for c in range(2):
                start = pl.multiple_of(c * n_all + source * n_seg, n_seg)
                mt_ref[j, pl.ds(start, n_seg), :] = pieces[h][j, c]
        m = mt_ref[j]
        g = dot3(m, m * vol_ref[...], ((1,), (1,)))
        g11, g21, g22 = g[:n_all, :n_all], g[n_all:, :n_all], g[n_all:, n_all:]
        packed[j, :n_all, :] = g21
        packed[j, n_all : 2 * n_all, :] = jnp.where(row >= col, g11, g22)
        diagonal = jnp.sum(jnp.where(row == col, g22, 0.0), axis=0, keepdims=True)
        packed[j, 2 * n_all :, :] = jnp.broadcast_to(diagonal, (8, n_all))
    mine_ref[...] = packed[core]
    other_ref[...] = packed[1 - core]


def gram(volumes, pieces):
    nj, two, n_seg, n_x = pieces[0].shape
    n = two * n_seg * len(HOPS)
    part = (n + 8, n // 2)
    return pl.pallas_call(
        gram_kernel,
        out_shape=[
            jax.ShapeDtypeStruct((nj, n, n_x), jnp.float32),
            jax.ShapeDtypeStruct(part, jnp.float32),
            jax.ShapeDtypeStruct(part, jnp.float32),
        ],
        in_specs=[IN_VMEM] * (1 + len(HOPS)),
        out_specs=[IN_VMEM] * 3,
        scratch_shapes=[pltpu.VMEM((nj,) + part, jnp.float32)],
        compiler_params=pltpu.CompilerParams(vmem_limit_bytes=16 << 20),
        cost_estimate=SMALL,
    )(volumes.reshape(1, n_x), *pieces)


def space_pairs(kind):
    pairs = []
    for i in range(32):
        y, x, core = i // 8, i // 2 % 4, i % 2
        if kind == "core":
            core = 1 - core
        else:
            along_x = (kind < 2) == (core == 0)
            flip = (lambda v: v ^ 1) if kind % 2 == 0 else (lambda v: 3 - v)
            x, y = (flip(x), y) if along_x else (x, flip(y))
        pairs.append((i, (y * 4 + x) * 2 + core))
    return pairs


def swap(value, kind):
    return lax.ppermute(value, "space", space_pairs(kind))


def add_steps(value, steps):
    for kind in steps:
        value = value + swap(value, kind)
    return value


def factor(work, begin, end):
    n = work.shape[0]
    rows = lax.broadcasted_iota(jnp.int32, (8, 128), 0)
    n_sub, half = PANEL // 8, n // 128
    for base in range(begin * PANEL, end * PANEL, PANEL):
        tile, lane = base // 128, base % 128
        tiles = [
            t for t in range(2 * half)
            if (tile <= t < half) or (t >= half and (t - half) * 128 < base + PANEL)
        ]
        live = [
            {t: work[base + 8 * i : base + 8 * i + 8, 128 * t : 128 * t + 128] for t in tiles}
            for i in range(n_sub)
        ]
        done = [{} for _ in range(n_sub)]
        column = [
            {
                j: jnp.broadcast_to(live[i][tile][:, lane + j : lane + j + 1], (8, 128))
                for j in range(8 * i + 8)
            }
            for i in range(n_sub)
        ]
        for p in range(PANEL):
            ip, sp = p // 8, p % 8
            pivot = jnp.broadcast_to(column[ip][p][sp : sp + 1, :], (8, 128))
            root = lax.rsqrt(pivot)
            inv = root * root
            mult = {i: column[i][p] * inv for i in range(ip, n_sub)}
            for j in range(p + 1, PANEL):
                ij = j // 8
                entry = jnp.broadcast_to(column[ij][p][j % 8 : j % 8 + 1, :], (8, 128))
                for i in range(ij, n_sub):
                    column[i][j] = column[i][j] - mult[i] * entry
            for t in tiles:
                row = jnp.broadcast_to(live[ip][t][sp : sp + 1, :], (8, 128))
                scaled = row * root
                done[ip][t] = scaled if sp == 0 else jnp.where(rows == sp, scaled, done[ip][t])
                for i in range(ip, n_sub):
                    if i > ip or sp < 7:
                        live[i][t] = live[i][t] - mult[i] * row
        for i in range(n_sub):
            for t in tiles:
                work[base + 8 * i : base + 8 * i + 8, 128 * t : 128 * t + 128] = done[i][t]
        after = base + PANEL
        if after < n:
            first = after // 128
            spans = ((128 * first, n), (n, n + (after + 127) // 128 * 128))
            right = [stacked(work[base:after, c0:c1], 1) for c0, c1 in spans]
            ends = [after + PANEL, n] if after + PANEL < n else [n]
            left = {
                blk: stacked(work[base:after, 128 * blk : 128 * blk + 128], 0)
                for blk in range(first, half)
            }
            for r0, r1 in zip([after] + ends, ends):
                for blk in range(r0 // 128, (r1 + 127) // 128):
                    lo, hi = max(r0, 128 * blk), min(r1, 128 * blk + 128)
                    part = left[blk][lo - 128 * blk : hi - 128 * blk, :]
                    for (c0, c1), other in zip(spans, right):
                        work[lo:hi, c0:c1] = work[lo:hi, c0:c1] - dot(part, other, ((1,), (0,)))


def stacked(value, side):
    parts = []
    for _ in range(3):
        parts.append(value.astype(jnp.bfloat16).astype(jnp.float32))
        value = value - parts[-1]
    chosen = [parts[pair[side]] for pair in PAIRS]
    both = jnp.concatenate(chosen, axis=0)
    if side == 0:
        both = both.T
    return both.astype(jnp.bfloat16)


def load_gram(work, packed):
    n = work.shape[0]
    h = n // 2
    row = lax.broadcasted_iota(jnp.int32, (h, h), 0)
    col = lax.broadcasted_iota(jnp.int32, (h, h), 1)
    g21, square = packed[:h, :], packed[h:n, :]
    turned = square.T
    work[:h, :h] = jnp.where(row >= col, square, turned)
    work[:h, h:n] = g21.T
    work[h:, :h] = g21
    g22 = jnp.where(row < col, square, turned)
    work[h:, h:n] = jnp.where(row == col, packed[n : n + 1, :], g22)
    row = lax.broadcasted_iota(jnp.int32, (n, n), 0)
    col = lax.broadcasted_iota(jnp.int32, (n, n), 1)
    work[:, n:] = jnp.where(row == col, 1.0, 0.0)


def factor_kernel(begin, end, in_ref, out_ref, work):
    n = work.shape[0]
    if begin == 0:
        load_gram(work, in_ref)
    else:
        work[...] = in_ref[...]
    factor(work, begin, end)
    if end * PANEL < n:
        out_ref[...] = work[...]
    else:
        row = lax.broadcasted_iota(jnp.int32, (n, n), 0)
        col = lax.broadcasted_iota(jnp.int32, (n, n), 1)
        out_ref[0] = jnp.where(row <= col, work[:, :n], 0.0)
        out_ref[1] = jnp.where(row >= col, work[:, n:], 0.0)


def factor_call(value, cuts):
    n = 2 * value.shape[1]
    ends = tuple(cuts) + (n // PANEL,)
    for begin, end in zip((0,) + ends, ends):
        last = end * PANEL == n
        value = pl.pallas_call(
            functools.partial(factor_kernel, begin, end),
            out_shape=jax.ShapeDtypeStruct((2, n, n) if last else (n, 2 * n), jnp.float32),
            in_specs=[IN_VMEM],
            out_specs=IN_VMEM,
            scratch_shapes=[pltpu.VMEM((n, 2 * n), jnp.float32)],
            compiler_params=pltpu.CompilerParams(vmem_limit_bytes=8 << 20),
            cost_estimate=pl.CostEstimate(
                flops=(end - begin) << 29, bytes_accessed=1000, transcendentals=0
            ),
        )(value)
    return value


def modes_kernel(js, root_rows, mine_ref, other_ref, mt_ref, *refs):
    modes_ref, tri_ref, inverse, held, tri, sems, tri_sems = refs[-7:]
    core = lax.rem(lax.axis_index("space"), 2)
    n_parts, part = held.shape[1], held.shape[2]

    def tri_copy(i):
        return pltpu.make_async_copy(tri.at[i], tri_ref.at[js[i]], tri_sems.at[i])

    def modes_copy(i, q):
        rows = pl.ds(q * part, part)
        return pltpu.make_async_copy(held.at[i, q], modes_ref.at[js[i], rows, :], sems.at[i, q])

    for i in range(len(js)):

        @pl.when(core == i)
        def _():
            tri[i] = mine_ref[0] * (1.0 / root_rows)
            inverse[i] = mine_ref[1] * root_rows

        @pl.when(core != i)
        def _():
            tri[i] = other_ref[0] * (1.0 / root_rows)
            inverse[i] = other_ref[1] * root_rows

        tri_copy(i).start()
    for i in range(len(js)):
        for q in range(n_parts):
            rows = slice(q * part, q * part + part)
            held[i, q] = dot3(mt_ref[i, :, rows], inverse[i], ((0,), (1,)))
            modes_copy(i, q).start()
    for i in range(len(js)):
        tri_copy(i).wait()
        for q in range(n_parts):
            modes_copy(i, q).wait()


def modes_call(js, n_local, root_rows, mine, other, mt, before):
    nj, n, n_x = mt.shape
    parts = 4
    before = list(before)
    return pl.pallas_call(
        functools.partial(modes_kernel, js, root_rows),
        out_shape=[
            jax.ShapeDtypeStruct((n_local, n_x, n), jnp.float32),
            jax.ShapeDtypeStruct((n_local, n, n), jnp.float32),
        ],
        in_specs=[IN_VMEM] * 3 + [IN_HBM] * len(before),
        out_specs=[IN_HBM, IN_HBM],
        scratch_shapes=[
            pltpu.VMEM((nj, n, n), jnp.float32),
            pltpu.VMEM((nj, parts, n_x // parts, n), jnp.float32),
            pltpu.VMEM((nj, n, n), jnp.float32),
            pltpu.SemaphoreType.DMA((nj, parts)),
            pltpu.SemaphoreType.DMA((nj,)),
        ],
        input_output_aliases={3 + i: i for i in range(len(before))},
        compiler_params=pltpu.CompilerParams(vmem_limit_bytes=16 << 20),
        cost_estimate=SMALL,
    )(mine, other, mt, *before)


def on_device(segments, volumes, freq_bins):
    n_freq = lax.axis_size("freq")
    n_local = freq_bins.shape[0] // n_freq
    root_rows = math.sqrt(segments.shape[2] * lax.axis_size("space"))
    sent = transform(freq_bins, segments)
    arrived = []
    for pieces in sent:
        got = [pieces[0]]
        for h, hop in enumerate(HOPS):
            if hop == 0:
                continue
            piece = pieces[h]
            if arrived:
                piece, arrived[-1][h] = lax.optimization_barrier((piece, arrived[-1][h]))
            got.append(lax.ppermute(piece, "freq", [(i, (i + hop) % n_freq) for i in range(n_freq)]))
        arrived.append(got)
    mt_first, mine, other = gram(volumes, arrived[0])
    first = add_steps(mine + swap(other, "core"), (0, 1))
    first, volumes = lax.optimization_barrier((first, volumes))
    mt_second, mine, other = gram(volumes, arrived[1])
    both = add_steps(jnp.stack([first, mine + swap(other, "core")]), (2, 3))
    second = add_steps(both[1], (0, 1))
    outs = ()
    for js, mt, value, cuts in ((GROUPS[0], mt_first, both[0], CUTS), (GROUPS[1], mt_second, second, ())):
        value = factor_call(value, cuts)
        outs = modes_call(js, n_local, root_rows, value, swap(value, "core"), mt, outs)
    return tuple(outs)


def solution(mesh):
    placed = (P("freq", None, "space"), P("space"), P())
    return jax.shard_map(
        on_device,
        mesh=mesh,
        in_specs=placed,
        out_specs=(P("freq", "space", None), P("freq", None, None)),
        check_vma=False,
    )
```

```python
import functools
import math

import jax
import jax.numpy as jnp
from jax import lax
from jax.experimental import pallas as pl
from jax.experimental.pallas import tpu as pltpu
from jax.sharding import PartitionSpec as P

HIGHEST = lax.Precision.HIGHEST
HOPS = (0, 2, 1, 3)
GROUPS = ((0, 1), (2, 3))
PANEL = 32
PAIRS = ((0, 0), (0, 1), (1, 0), (0, 2), (2, 0), (1, 1))
CUTS = (4,)
IN_VMEM = pl.BlockSpec(memory_space=pltpu.VMEM)
IN_HBM = pl.BlockSpec(memory_space=pltpu.HBM)
SMALL = pl.CostEstimate(flops=1000, bytes_accessed=1000, transcendentals=0)


def dot(a, b, dims, precision=None):
    return lax.dot_general(
        a, b, (dims, ((), ())), precision=precision, preferred_element_type=jnp.float32
    )


def dot3(a, b, dims):
    ah, bh = a.astype(jnp.bfloat16), b.astype(jnp.bfloat16)
    al = (a - ah.astype(jnp.float32)).astype(jnp.bfloat16)
    bl = (b - bh.astype(jnp.float32)).astype(jnp.bfloat16)
    return dot(ah, bh, dims) + (dot(ah, bl, dims) + dot(al, bh, dims))


def transform_kernel(bins_in, seg_ref, *refs):
    outs, (table, landing, held, sems, bins_ref, bins_sem) = refs[:-6], refs[-6:]
    n_seg, fft_len = seg_ref.shape[0], seg_ref.shape[1]
    group, n_rows = 8, table.shape[0]
    per_hop = n_rows // len(HOPS)
    n_local = per_hop // 2

    batch = 4

    def segment_copy(b):
        some = pl.ds(b * batch, batch)
        return pltpu.make_async_copy(seg_ref.at[some], held.at[some], sems.at[b])

    bins_copy = pltpu.make_async_copy(bins_in, bins_ref, bins_sem)
    bins_copy.start()
    for b in range(n_seg // batch):
        segment_copy(b).start()
    me = lax.axis_index("freq")
    row = lax.broadcasted_iota(jnp.int32, (n_rows, fft_len), 0)
    step = lax.broadcasted_iota(jnp.int32, (n_rows, fft_len), 1)
    bins = jnp.zeros((n_rows, fft_len), jnp.int32)
    bins_copy.wait()
    for h, hop in enumerate(HOPS):
        home = lax.rem(me + hop, len(HOPS))
        for j in range(n_local):
            which = bins_ref[home * n_local + j]
            bins = jnp.where(row // 2 == h * n_local + j, which, bins)
    phase = lax.rem(bins * step, fft_len)
    angle = 2.0 * math.pi / fft_len * phase.astype(jnp.float32)
    window = 0.5 - 0.5 * jnp.cos(2.0 * math.pi / fft_len * step.astype(jnp.float32))
    scale = window / math.sqrt(fft_len)
    wave = jnp.where(lax.rem(row, 2) == 0, jnp.cos(angle), -jnp.sin(angle))
    table[...] = (scale * wave).astype(jnp.bfloat16)

    @pl.loop(0, n_seg // group)
    def _(g):
        base = pl.multiple_of(g * group, group)
        for b in range(group):
            if b % batch == 0:
                segment_copy(g * (group // batch) + b // batch).wait()
            sums = dot(table[...], held[base + b], ((1,), (0,)))
            for k in range(landing.shape[0]):
                tile = slice(128 * k, 128 * k + 128)
                landing[k, pl.ds(b, n_rows, stride=group), :] = sums[:, tile]
        n = 0
        for js in GROUPS:
            for h in range(len(HOPS)):
                for i, j in enumerate(js):
                    for c in range(2):
                        r = (h * per_hop + j * 2 + c) * group
                        for k in range(landing.shape[0]):
                            tile = slice(128 * k, 128 * k + 128)
                            outs[n][i, c, pl.ds(base, group), tile] = landing[k, r : r + group, :]
                n += 1


def transform(bins, segments):
    n_seg, fft_len, n_x = segments.shape
    n_rows = 2 * bins.shape[0]
    shapes = [
        jax.ShapeDtypeStruct((len(js), 2, n_seg, n_x), jnp.float32)
        for js in GROUPS
        for _ in HOPS
    ]
    outs = pl.pallas_call(
        transform_kernel,
        out_shape=shapes,
        in_specs=[IN_HBM, IN_HBM],
        out_specs=[IN_VMEM] * len(shapes),
        scratch_shapes=[
            pltpu.VMEM((n_rows, fft_len), jnp.bfloat16),
            pltpu.VMEM((n_x // 128, n_rows * 8, 128), jnp.float32),
            pltpu.VMEM(segments.shape, segments.dtype),
            pltpu.SemaphoreType.DMA((n_seg,)),
            pltpu.SMEM(bins.shape, bins.dtype),
            pltpu.SemaphoreType.DMA,
        ],
        compiler_params=pltpu.CompilerParams(vmem_limit_bytes=50 << 20),
        cost_estimate=SMALL,
    )(bins, segments)
    k = len(HOPS)
    return [outs[i * k : (i + 1) * k] for i in range(len(GROUPS))]


def gram_kernel(vol_ref, *refs):
    pieces, (mt_ref, mine_ref, other_ref, packed) = refs[:4], refs[4:]
    me, core = lax.axis_index("freq"), lax.rem(lax.axis_index("space"), 2)
    n_seg = pieces[0].shape[2]
    n_all = n_seg * len(HOPS)
    row = lax.broadcasted_iota(jnp.int32, (n_all, n_all), 0)
    col = lax.broadcasted_iota(jnp.int32, (n_all, n_all), 1)
    for j in range(mt_ref.shape[0]):
        for h, hop in enumerate(HOPS):
            source = lax.rem(me + len(HOPS) - hop, len(HOPS))
            for c in range(2):
                start = pl.multiple_of(c * n_all + source * n_seg, n_seg)
                mt_ref[j, pl.ds(start, n_seg), :] = pieces[h][j, c]
        m = mt_ref[j]
        m = m * jnp.sqrt(vol_ref[...])
        high = m.astype(jnp.bfloat16)
        low = (m - high.astype(jnp.float32)).astype(jnp.bfloat16)
        mixed = dot(high, low, ((1,), (1,)))
        g = dot(high, high, ((1,), (1,))) + (mixed + mixed.T)
        g11, g21, g22 = g[:n_all, :n_all], g[n_all:, :n_all], g[n_all:, n_all:]
        packed[j, :n_all, :] = g21
        packed[j, n_all : 2 * n_all, :] = jnp.where(row >= col, g11, g22)
        diagonal = jnp.sum(jnp.where(row == col, g22, 0.0), axis=0, keepdims=True)
        packed[j, 2 * n_all :, :] = jnp.broadcast_to(diagonal, (8, n_all))
    mine_ref[...] = packed[core]
    other_ref[...] = packed[1 - core]


def gram(volumes, pieces):
    nj, two, n_seg, n_x = pieces[0].shape
    n = two * n_seg * len(HOPS)
    part = (n + 8, n // 2)
    return pl.pallas_call(
        gram_kernel,
        out_shape=[
            jax.ShapeDtypeStruct((nj, n, n_x), jnp.float32),
            jax.ShapeDtypeStruct(part, jnp.float32),
            jax.ShapeDtypeStruct(part, jnp.float32),
        ],
        in_specs=[IN_VMEM] * (1 + len(HOPS)),
        out_specs=[IN_VMEM] * 3,
        scratch_shapes=[pltpu.VMEM((nj,) + part, jnp.float32)],
        compiler_params=pltpu.CompilerParams(vmem_limit_bytes=16 << 20),
        cost_estimate=SMALL,
    )(volumes.reshape(1, n_x), *pieces)


def space_pairs(kind):
    pairs = []
    for i in range(32):
        y, x, core = i // 8, i // 2 % 4, i % 2
        if kind == "core":
            core = 1 - core
        else:
            along_x = (kind < 2) == (core == 0)
            flip = (lambda v: v ^ 1) if kind % 2 == 0 else (lambda v: 3 - v)
            x, y = (flip(x), y) if along_x else (x, flip(y))
        pairs.append((i, (y * 4 + x) * 2 + core))
    return pairs


def swap(value, kind):
    return lax.ppermute(value, "space", space_pairs(kind))


def add_steps(value, steps):
    for kind in steps:
        value = value + swap(value, kind)
    return value


def factor(work, begin, end):
    n = work.shape[0]
    rows = lax.broadcasted_iota(jnp.int32, (8, 128), 0)
    n_sub, half = PANEL // 8, n // 128
    for base in range(begin * PANEL, end * PANEL, PANEL):
        tile, lane = base // 128, base % 128
        tiles = [
            t for t in range(2 * half)
            if (tile <= t < half) or (t >= half and (t - half) * 128 < base + PANEL)
        ]
        live = [
            {t: work[base + 8 * i : base + 8 * i + 8, 128 * t : 128 * t + 128] for t in tiles}
            for i in range(n_sub)
        ]
        done = [{} for _ in range(n_sub)]
        column = [
            {
                j: jnp.broadcast_to(live[i][tile][:, lane + j : lane + j + 1], (8, 128))
                for j in range(8 * i + 8)
            }
            for i in range(n_sub)
        ]
        for p in range(PANEL):
            ip, sp = p // 8, p % 8
            pivot = jnp.broadcast_to(column[ip][p][sp : sp + 1, :], (8, 128))
            root = lax.rsqrt(pivot)
            inv = root * root
            mult = {i: column[i][p] * inv for i in range(ip, n_sub)}
            for j in range(p + 1, PANEL):
                ij = j // 8
                entry = jnp.broadcast_to(column[ij][p][j % 8 : j % 8 + 1, :], (8, 128))
                for i in range(ij, n_sub):
                    column[i][j] = column[i][j] - mult[i] * entry
            for t in tiles:
                row = jnp.broadcast_to(live[ip][t][sp : sp + 1, :], (8, 128))
                scaled = row * root
                done[ip][t] = scaled if sp == 0 else jnp.where(rows == sp, scaled, done[ip][t])
                for i in range(ip, n_sub):
                    if i > ip or sp < 7:
                        live[i][t] = live[i][t] - mult[i] * row
        for i in range(n_sub):
            for t in tiles:
                work[base + 8 * i : base + 8 * i + 8, 128 * t : 128 * t + 128] = done[i][t]
        after = base + PANEL
        if after < n:
            first = after // 128
            spans = ((128 * first, n), (n, n + (after + 127) // 128 * 128))
            right = [stacked(work[base:after, c0:c1], 1) for c0, c1 in spans]
            ends = [after + PANEL, n] if after + PANEL < n else [n]
            left = {
                blk: stacked(work[base:after, 128 * blk : 128 * blk + 128], 0)
                for blk in range(first, half)
            }
            for r0, r1 in zip([after] + ends, ends):
                for blk in range(r0 // 128, (r1 + 127) // 128):
                    lo, hi = max(r0, 128 * blk), min(r1, 128 * blk + 128)
                    part = left[blk][lo - 128 * blk : hi - 128 * blk, :]
                    for (c0, c1), other in zip(spans, right):
                        work[lo:hi, c0:c1] = work[lo:hi, c0:c1] - dot(part, other, ((1,), (0,)))


def stacked(value, side):
    parts = []
    for _ in range(3):
        parts.append(value.astype(jnp.bfloat16).astype(jnp.float32))
        value = value - parts[-1]
    chosen = [parts[pair[side]] for pair in PAIRS]
    both = jnp.concatenate(chosen, axis=0)
    if side == 0:
        both = both.T
    return both.astype(jnp.bfloat16)


def load_gram(work, packed):
    n = work.shape[0]
    h = n // 2
    row = lax.broadcasted_iota(jnp.int32, (h, h), 0)
    col = lax.broadcasted_iota(jnp.int32, (h, h), 1)
    g21, square = packed[:h, :], packed[h:n, :]
    turned = square.T
    work[:h, :h] = jnp.where(row >= col, square, turned)
    work[:h, h:n] = g21.T
    work[h:, :h] = g21
    g22 = jnp.where(row < col, square, turned)
    work[h:, h:n] = jnp.where(row == col, packed[n : n + 1, :], g22)
    row = lax.broadcasted_iota(jnp.int32, (n, n), 0)
    col = lax.broadcasted_iota(jnp.int32, (n, n), 1)
    work[:, n:] = jnp.where(row == col, 1.0, 0.0)


def factor_kernel(begin, end, in_ref, out_ref, work):
    n = work.shape[0]
    if begin == 0:
        load_gram(work, in_ref)
    else:
        work[...] = in_ref[...]
    factor(work, begin, end)
    if end * PANEL < n:
        out_ref[...] = work[...]
    else:
        row = lax.broadcasted_iota(jnp.int32, (n, n), 0)
        col = lax.broadcasted_iota(jnp.int32, (n, n), 1)
        out_ref[0] = jnp.where(row <= col, work[:, :n], 0.0)
        out_ref[1] = jnp.where(row >= col, work[:, n:], 0.0)


def factor_call(value, cuts):
    n = 2 * value.shape[1]
    ends = tuple(cuts) + (n // PANEL,)
    for begin, end in zip((0,) + ends, ends):
        last = end * PANEL == n
        value = pl.pallas_call(
            functools.partial(factor_kernel, begin, end),
            out_shape=jax.ShapeDtypeStruct((2, n, n) if last else (n, 2 * n), jnp.float32),
            in_specs=[IN_VMEM],
            out_specs=IN_VMEM,
            scratch_shapes=[pltpu.VMEM((n, 2 * n), jnp.float32)],
            compiler_params=pltpu.CompilerParams(vmem_limit_bytes=8 << 20),
            cost_estimate=pl.CostEstimate(
                flops=(end - begin) << 29, bytes_accessed=1000, transcendentals=0
            ),
        )(value)
    return value


def modes_kernel(js, root_rows, mine_ref, other_ref, mt_ref, *refs):
    modes_ref, tri_ref, inverse, held, tri, sems, tri_sems = refs[-7:]
    core = lax.rem(lax.axis_index("space"), 2)
    n_parts, part = held.shape[1], held.shape[2]

    def tri_copy(i):
        return pltpu.make_async_copy(tri.at[i], tri_ref.at[js[i]], tri_sems.at[i])

    def modes_copy(i, q):
        rows = pl.ds(q * part, part)
        return pltpu.make_async_copy(held.at[i, q], modes_ref.at[js[i], rows, :], sems.at[i, q])

    for i in range(len(js)):

        @pl.when(core == i)
        def _():
            tri[i] = mine_ref[0] * (1.0 / root_rows)
            inverse[i] = mine_ref[1] * root_rows

        @pl.when(core != i)
        def _():
            tri[i] = other_ref[0] * (1.0 / root_rows)
            inverse[i] = other_ref[1] * root_rows

        tri_copy(i).start()
    for i in range(len(js)):
        for q in range(n_parts):
            rows = slice(q * part, q * part + part)
            held[i, q] = dot3(mt_ref[i, :, rows], inverse[i], ((0,), (1,)))
            modes_copy(i, q).start()
    for i in range(len(js)):
        tri_copy(i).wait()
        for q in range(n_parts):
            modes_copy(i, q).wait()


def modes_call(js, n_local, root_rows, mine, other, mt, before):
    nj, n, n_x = mt.shape
    parts = 4
    before = list(before)
    return pl.pallas_call(
        functools.partial(modes_kernel, js, root_rows),
        out_shape=[
            jax.ShapeDtypeStruct((n_local, n_x, n), jnp.float32),
            jax.ShapeDtypeStruct((n_local, n, n), jnp.float32),
        ],
        in_specs=[IN_VMEM] * 3 + [IN_HBM] * len(before),
        out_specs=[IN_HBM, IN_HBM],
        scratch_shapes=[
            pltpu.VMEM((nj, n, n), jnp.float32),
            pltpu.VMEM((nj, parts, n_x // parts, n), jnp.float32),
            pltpu.VMEM((nj, n, n), jnp.float32),
            pltpu.SemaphoreType.DMA((nj, parts)),
            pltpu.SemaphoreType.DMA((nj,)),
        ],
        input_output_aliases={3 + i: i for i in range(len(before))},
        compiler_params=pltpu.CompilerParams(vmem_limit_bytes=16 << 20),
        cost_estimate=SMALL,
    )(mine, other, mt, *before)


def on_device(segments, volumes, freq_bins):
    n_freq = lax.axis_size("freq")
    n_local = freq_bins.shape[0] // n_freq
    root_rows = math.sqrt(segments.shape[2] * lax.axis_size("space"))
    sent = transform(freq_bins, segments)
    arrived = []
    for pieces in sent:
        got = [pieces[0]]
        for h, hop in enumerate(HOPS):
            if hop == 0:
                continue
            piece = pieces[h]
            if arrived:
                piece, arrived[-1][h] = lax.optimization_barrier((piece, arrived[-1][h]))
            got.append(lax.ppermute(piece, "freq", [(i, (i + hop) % n_freq) for i in range(n_freq)]))
        arrived.append(got)
    mt_first, mine, other = gram(volumes, arrived[0])
    first = add_steps(mine + swap(other, "core"), (0, 1))
    first, volumes = lax.optimization_barrier((first, volumes))
    mt_second, mine, other = gram(volumes, arrived[1])
    both = add_steps(jnp.stack([first, mine + swap(other, "core")]), (2, 3))
    second = add_steps(both[1], (0, 1))
    outs = ()
    for js, mt, value, cuts in ((GROUPS[0], mt_first, both[0], CUTS), (GROUPS[1], mt_second, second, ())):
        value = factor_call(value, cuts)
        outs = modes_call(js, n_local, root_rows, value, swap(value, "core"), mt, outs)
    return tuple(outs)


def solution(mesh):
    placed = (P("freq", None, "space"), P("space"), P())
    return jax.shard_map(
        on_device,
        mesh=mesh,
        in_specs=placed,
        out_specs=(P("freq", "space", None), P("freq", None, None)),
        check_vma=False,
    )
```
